128 devices in a mesh: cls: 16 (over y, z_hi, core), feat: 8 (over z_lo, x).
Axes of the slice: x: 4, y: 4, z: 4 (z_hi: 2, z_lo: 2; z = z_hi * 2 + z_lo), core: 2. Of those that a mesh axis runs over, the one named last changes fastest.
Arguments:
- embeddings: bfloat16 [16384, 4608], P(('cls', 'feat')), may hold values from -6 to 6
- labels: int32 [16384, 1], P(('cls', 'feat')), may hold values from 0 to 15; in each aligned block of 128 rows (0 to 127, 128 to 255, ...) at most 16 rows name the same one
- previous: float32 [16, 4608, 1152], P('cls', 'feat'), as said below
Outputs:
- class_cov: float32 [16, 4608, 4608], P('cls', None, 'feat')
- panel_factor: float32 [16, 4608, 1152], P('cls', 'feat')
The draws below stay inside these ranges and needn't reach their ends.
Inputs may be any that keep to these rules, and one draw needn't show every extreme that they name: `labels`: among the rows of one device no class has more than 16 rows, and on every device some class has exactly 16; every class has a row somewhere. For every class the first 1152 rows of previous form a symmetric positive definite matrix whose smallest eigenvalue is at least 0.05.
All inputs are finite; a program needn't handle non-finite values.
Results may differ from the reference program's by a relative error of at most 0.0003.
Values may be sent and summed in bfloat16 or wider, within the bound.
A program may use at most 192 MiB of HBM per device.

```python
import math
import jax
import jax.numpy as jnp
import numpy as np
from jax import lax

D = 4608
PANEL = 1152
ROWS_DEV = 128
CLASSES = 16
CAP = 16
ROWS = 16384
DEVICES = 128


def square_block(factor_rows):
    product = jnp.dot(factor_rows, factor_rows.T, precision=lax.Precision.HIGHEST)
    product = 0.5 * (product + product.T) / (2.0 * PANEL)
    index = jnp.arange(PANEL, dtype=jnp.int32)
    on_diag = index[:, None] == index[None, :]
    return product + jnp.where(on_diag, 0.05, 0.0).astype(jnp.float32)


def draw_previous(key, part):
    key = jax.random.fold_in(key, 7)
    k_low = jax.random.fold_in(key, 1)
    k_fac = jax.random.fold_in(key, 2)
    rest_rows = D - PANEL
    lower = jax.random.normal(k_low, (CLASSES, rest_rows, PANEL), jnp.float32)
    factors = jax.random.normal(k_fac, (CLASSES, PANEL, 2 * PANEL), jnp.float32)
    top = lax.map(square_block, factors)
    return jnp.concatenate([top, lower], axis=1).astype(jnp.float32)


def block_levels(rng, shape, split, least, top_value):
    def one(dim, shards_of):
        steps = jax.random.uniform(jax.random.fold_in(jax.random.fold_in(rng, 6), dim), (shards_of,), jnp.float32, least / len(split), top_value / len(split))
        return jnp.repeat(jnp.exp(steps), shape[dim] // shards_of).reshape((-1,) + (1,) * (len(shape) - dim - 1))

    factor_of = one(*split[0])
    for cut in split[1:]:
        factor_of = factor_of * one(*cut)
    return factor_of


def routed_block(own_key, own, number, rows, amount, top, bound, lean):
    ranking = jax.random.permutation(own_key, amount)
    packed, usual = load_shares(amount, rows * top, bound, lean, True), load_shares(amount, rows * top, bound, lean, False)
    places = jnp.arange(amount)

    def named(lengths, offset_by):
        used = int((lengths > 0).sum())
        fixed = max(1, used // 4)
        passed = fixed + (places - fixed + offset_by * (used - fixed)) % max(1, amount - fixed)
        return jnp.zeros((amount,), jnp.int32).at[ranking[jnp.where(places < fixed, places, passed)]].set(jnp.asarray(lengths, jnp.int32))

    lengths = jnp.where(number % 4 == 0, named(packed, number // 4), named(usual, number - number // 4 - 1))
    mixed = jax.random.permutation(jax.random.fold_in(own, 3), amount)
    donor, receiver = mixed[0:amount // 2 * 2:2], mixed[1:amount // 2 * 2:2]
    margin = jnp.minimum(lengths[donor] - 1, bound - lengths[receiver]) // 2
    margin = jnp.where((donor == ranking[0]) | (receiver == ranking[0]) | (lengths[receiver] == 0), 0, jnp.maximum(margin, 0))
    passed = jax.random.randint(jax.random.fold_in(own, 4), (amount // 2,), 0, 1 << 20) % (margin + 1)
    lengths = lengths.at[donor].add(-passed).at[receiver].add(passed)
    items = jnp.searchsorted(jnp.cumsum(lengths), jnp.arange(rows * top), side="right").astype(jnp.int32)
    grid = items.reshape(top, rows).T
    grid = grid[jax.random.permutation(jax.random.fold_in(own, 1), rows)]
    offset_by = jax.random.randint(jax.random.fold_in(own, 2), (rows, 1), 0, top)
    return jnp.take_along_axis(grid, (jnp.arange(top)[None, :] + offset_by) % top, axis=1)


def load_shares(number_of, total, bound, lean, full):
    portions = [(1 << 20) // math.isqrt(rank ** lean) + 1 for rank in range(1, number_of + 1)]
    largest = bound if full else min(bound, max(-(-total // number_of), total * portions[0] // sum(portions)))
    least = 1 if total - largest >= number_of - 1 else 0
    given, spare = [largest] + [least] * (number_of - 1), total - largest - least * (number_of - 1)
    while spare > 0:
        movable = [i for i in range(1, number_of) if given[i] < largest] or [i for i in range(1, number_of) if given[i] < bound]
        pool, budget = sum([portions[i] for i in movable]), spare
        for i in movable:
            extra = min(bound - given[i], max(1, budget * portions[i] // pool), spare)
            given[i] = given[i] + extra
            spare = spare - extra
    return np.array(given)


def gaussian(rng, extent, spread, reach, pieces=(), kind=jnp.bfloat16):
    drawn = jax.random.normal(rng, extent, jnp.float32) * spread
    if len(pieces) > 0:
        drawn = block_levels(rng, extent, pieces, -0.22, 0.18) * drawn
    return jnp.clip(drawn, min=-reach, max=reach).astype(kind)


def setup_inputs(seed: int = 0) -> dict:
    key_of = jax.random.split(jax.random.key(seed), 4)
    embeddings = gaussian(key_of[0], (ROWS, D), 1.0, 6.0, ((0, 128),))
    labels_keys = jax.random.split(jax.random.fold_in(key_of[1], 1), ROWS // ROWS_DEV)
    labels_turns = jax.random.permutation(jax.random.fold_in(key_of[1], 3), ROWS // ROWS_DEV)
    labels = jax.vmap(lambda own, number: routed_block(jax.random.fold_in(key_of[1], 2), own, number, ROWS_DEV, CLASSES, 1, CAP, 2))(labels_keys, labels_turns).reshape((ROWS, 1))
    previous = draw_previous(jax.random.fold_in(key_of[3], 71), 0)
    return {"embeddings": embeddings, "labels": labels, "previous": previous}


def one_class(klass, sorted_rows, sorted_labels, offsets):
    window = CAP * DEVICES
    start = jnp.minimum(offsets[klass], ROWS - window).astype(jnp.int32)
    block = lax.dynamic_slice(sorted_rows, (start, jnp.int32(0)), (window, D))
    chosen = lax.dynamic_slice(sorted_labels, (start,), (window,)) == klass
    weights = jnp.where(chosen, 1.0, 0.0).astype(jnp.float32)
    masked = block.astype(jnp.float32) * weights[:, None]
    gram = jnp.dot(masked.T, masked, precision=lax.Precision.HIGHEST)
    sums = jnp.sum(masked, axis=0)
    count = jnp.sum(weights)
    mean = sums / count
    return gram / count - mean[:, None] * mean[None, :]

def panel_one(block):
    lead = jnp.linalg.cholesky(block[:PANEL, :])
    return lax.linalg.triangular_solve(lead, block, left_side=False, lower=True, transpose_a=True)

def reference(embeddings, labels, previous):
    label_col = labels[:, 0].astype(jnp.int32)
    order = jnp.argsort(label_col, stable=True)
    sorted_rows = embeddings[order]
    sorted_labels = label_col[order]
    counts = jnp.sum((label_col[:, None] == jnp.arange(CLASSES, dtype=jnp.int32)[None, :]).astype(jnp.int32), axis=0)
    offsets = (jnp.cumsum(counts) - counts).astype(jnp.int32)
    class_cov = lax.map(lambda klass: one_class(klass, sorted_rows, sorted_labels, offsets), jnp.arange(CLASSES, dtype=jnp.int32))
    panel_factor = lax.map(panel_one, previous)
    return (class_cov, panel_factor)
```

```python
import functools

import jax
import jax.numpy as jnp
from jax import lax
from jax.experimental import pallas as pl
from jax.experimental.pallas import tpu as pltpu
from jax.sharding import PartitionSpec as P

MESH = pl.DeviceIdType.MESH
HI = lax.Precision.HIGHEST
D = 4608
CAP = 16
CLS = 16
FEAT = 8
PW = 2560
QW = D - PW
SLOT = CAP * CLS
HALF = SLOT // 2
TILE = D // FEAT
WIN = 640
PANEL = 1152
OWN = 576
ROWS = 1792
NB = 128
COLS = 384
NPAN = 3
PIECE = (144, 96, 48)
LPW = 128
LHS = TILE + 16


def dot_t(a, b):
    return lax.dot_general(a, b, (((1,), (1,)), ((), ())), precision=HI, preferred_element_type=jnp.float32)


def dot_ta(a, b):
    return lax.dot_general(a, b, (((0,), (0,)), ((), ())), precision=HI, preferred_element_type=jnp.float32)


def diag_inverse(W, r0, SA, SM):
    SA[...] = W[pl.ds(r0, NB), pl.ds(r0, NB)]
    row = lax.broadcasted_iota(jnp.int32, (NB, NB), 0)
    col = lax.broadcasted_iota(jnp.int32, (NB, NB), 1)
    SM[...] = jnp.where(row == col, 1.0, 0.0).astype(jnp.float32)
    sub = lax.broadcasted_iota(jnp.int32, (8, NB), 0)
    for g in range(NB // 8):
        lo = 8 * g
        pa = SA[lo : lo + 8, :]
        pm = SM[lo : lo + 8, :]
        cols = [jnp.broadcast_to(pa[:, lo + t : lo + t + 1], (8, NB)) for t in range(8)]
        scale = jnp.zeros((8, NB), jnp.float32)
        for t in range(8):
            piv = jnp.broadcast_to(cols[t][t : t + 1, :], (8, NB))
            m = jnp.where(sub > t, cols[t] * (1.0 / piv), 0.0)
            scale = jnp.where(sub == t, piv, scale)
            for u in range(t + 1, 8):
                cols[u] = cols[u] - m * jnp.broadcast_to(cols[u][t : t + 1, :], (8, NB))
            pa = pa - m * jnp.broadcast_to(pa[t : t + 1, :], (8, NB))
            pm = pm - m * jnp.broadcast_to(pm[t : t + 1, :], (8, NB))
        s = lax.rsqrt(scale)
        y = pa * s
        z = pm * s
        SM[lo : lo + 8, :] = z
        if g < NB // 8 - 1:
            n0 = lo + 8
            upd = dot_ta(y, jnp.concatenate([y, z], axis=1))
            SA[n0:, :] = SA[n0:, :] - upd[n0:, :NB]
            SM[n0:, :] = SM[n0:, :] - upd[n0:, NB:]


def chol_step(W, k, SA, SM, hook):
    r0 = pl.multiple_of(k * NB, NB)
    b = lax.rem(k, 3)
    s = k // 3
    for st in (1, 2):

        @pl.when((b == 0) & (s == st))
        def _():
            c0 = 384 * st

            def body(i, _):
                r = pl.multiple_of(c0 + i * 128, 128)
                acc = W[pl.ds(r, 128), c0 : c0 + 384]
                for q in range(st):
                    acc = acc - dot_t(
                        W[pl.ds(r, 128), 384 * q : 384 * q + 384], W[c0 : c0 + 384, 384 * q : 384 * q + 384]
                    )
                W[pl.ds(r, 128), c0 : c0 + 384] = acc
                return 0

            lax.fori_loop(0, (ROWS - c0) // 128, body, 0)

    diag_inverse(W, r0, SA, SM)
    hook(0)

    def tb(i, _):
        r = pl.multiple_of(i * 256, 256)
        W[pl.ds(r, 256), pl.ds(r0, NB)] = dot_t(W[pl.ds(r, 256), pl.ds(r0, NB)], SM[...])
        return 0

    lax.fori_loop((k + 1) // 2, ROWS // 256, tb, 0)
    for bb in (0, 1):

        @pl.when(b == bb)
        def _():
            n = 256 - 128 * bb

            def ub(i, _):
                r = pl.multiple_of(i * 256, 256)
                c1 = pl.multiple_of(r0 + NB, NB)
                W[pl.ds(r, 256), pl.ds(c1, n)] = W[pl.ds(r, 256), pl.ds(c1, n)] - dot_t(
                    W[pl.ds(r, 256), pl.ds(r0, NB)], W[pl.ds(c1, n), pl.ds(r0, NB)]
                )
                return 0

            lax.fori_loop((k + 1) // 2, ROWS // 256, ub, 0)


def kernel(
    stp, stq, cst, prev,
    gram, panel, ssum, tsum, cnt,
    GP, GQ, W, XT, TT, LT, SA, SM, C1, C2,
    p1r, p1s, lr, ls, lxs, lxr, lzs, lzr, xs, xr, zs, zr, ps, pr, cr, cs, own_sem,
):
    c = lax.axis_index("cls")
    f = lax.axis_index("feat")
    x = lax.rem(f, 4)
    zoff = f - x
    zmate = 4 - zoff
    mate = x + zmate
    zhi = lax.rem(c // 2, 2)

    def at_x(d, z):
        return z + lax.rem(x + d, 4)

    right, left, far = at_x(1, zoff), at_x(3, zoff), at_x(2, zoff)

    bar = pltpu.get_barrier_semaphore()

    def sig(cc, ff):
        pl.semaphore_signal(bar, inc=1, device_id=(cc, ff), device_id_type=MESH)

    def sig_cls(cc, _):
        @pl.when(cc != c)
        def _():
            sig(cc, f)

        sig(cc, mate)
        return 0

    lax.fori_loop(0, CLS, sig_cls, 0)
    for d in (1, 2, 3):
        sig(c, at_x(d, zoff))
        sig(c, at_x(d, zmate))
    pl.semaphore_wait(bar, 37)

    def put(src, dst, dev, ssem, rsem):
        pltpu.make_async_remote_copy(
            src_ref=src, dst_ref=dst, send_sem=ssem, recv_sem=rsem, device_id=dev, device_id_type=MESH
        ).start()

    def wait(ref, sem):
        pltpu.make_async_copy(ref, ref, sem).wait()

    def put_same(ref, ff, ssem, rsem):
        put(ref, ref, (c, ff), ssem, rsem)

    def piece(j, i, lo=0, hi=COLS):
        r = pl.multiple_of(COLS * j + PIECE[j] * i, 8)
        return W.at[pl.ds(r, PIECE[j]), COLS * j + lo : COLS * j + hi]

    for src in (0, 1):

        @pl.when(f == src)
        def _():
            for j in range(NPAN):
                for i in range(FEAT):
                    r = COLS * j + PIECE[j] * i
                    if r // OWN != src:
                        continue
                    r = r - OWN * src
                    ref = prev.at[r : r + PIECE[j], COLS * j : COLS * (j + 1)]
                    if i == src:
                        pltpu.make_async_copy(ref, piece(j, i), lr.at[j]).start()
                    else:
                        put(ref, piece(j, i), (c, i), ls.at[j], lr.at[j])

    own_copy = pltpu.make_async_copy(prev, W.at[PANEL : PANEL + OWN, :], own_sem)
    own_copy.start()

    def route(cc, _):
        same = lax.rem(cc // 2, 2) == zhi
        g = jnp.where(same, f, mate)
        r = pl.multiple_of(CAP * c, CAP)
        dq = GQ.at[g, pl.ds(r, CAP), :]

        @pl.when(cc == c)
        def _():
            pltpu.make_async_copy(stq.at[cc], dq, p1r.at[0]).start()
            pltpu.make_async_copy(cst.at[cc], C1.at[c], cr.at[0]).start()

        @pl.when(cc != c)
        def _():
            put(stq.at[cc], dq, (cc, g), p1s.at[0], p1r.at[0])
            put(cst.at[cc], C1.at[c], (cc, f), cs.at[0], cr.at[0])

        return 0

    lax.fori_loop(0, CLS, route, 0)

    def route_p(cc, _):
        same = lax.rem(cc // 2, 2) == zhi
        g = jnp.where(same, f, mate)
        r = pl.multiple_of(CAP * c, CAP)
        dp = GP.at[g, pl.ds(r, CAP), :]

        @pl.when(cc == c)
        def _():
            pltpu.make_async_copy(stp.at[cc], dp, p1r.at[1]).start()

        @pl.when(cc != c)
        def _():
            put(stp.at[cc], dp, (cc, g), p1s.at[1], p1r.at[1])

        return 0

    lax.fori_loop(0, CLS, route_p, 0)

    def zero(i, _):
        gram[:, pl.ds(pl.multiple_of(512 * i, 512), 512)] = jnp.zeros((TILE, 512), jnp.float32)
        return 0

    lax.fori_loop(0, D // 512, zero, 0)
    ssum[...] = jnp.zeros_like(ssum)
    tsum[...] = jnp.zeros_like(tsum)
    LT[TILE:, :] = jnp.ones((LHS - TILE, SLOT), jnp.bfloat16)
    W[PANEL + OWN :, :] = jnp.zeros((ROWS - PANEL - OWN, PANEL), jnp.float32)

    along_x = ((0, right), (1, left), (2, far))
    from_x = ((0, 3), (1, 1), (2, 2))

    def lead_a(j):
        wait(piece(j, f), lr.at[j])
        put_same(piece(j, f, 0, LPW), mate, lzs.at[j, 0], lzr.at[j, 0])
        for d, ff in along_x:
            put_same(piece(j, f), ff, lxs.at[j, d], lxr.at[j, d])
        put_same(piece(j, f, LPW), mate, lzs.at[j, 1], lzr.at[j, 1])

    def lead_b(j):
        wait(piece(j, mate, 0, LPW), lzr.at[j, 0])
        for d, ff in along_x:
            put_same(piece(j, mate, 0, LPW), ff, lxs.at[j, 3 + d], lxr.at[j, 3 + d])

    def lead_c(j):
        for d, off in from_x:
            wait(piece(j, at_x(off, zoff)), lxr.at[j, d])
            put_same(piece(j, at_x(off, zoff), LPW), mate, lzs.at[j, 2 + d], lzr.at[j, 2 + d])

    def lead_d(j):
        wait(piece(j, mate, LPW), lzr.at[j, 1])
        for d, off in from_x:
            wait(piece(j, at_x(off, zmate), 0, LPW), lxr.at[j, 3 + d])
            wait(piece(j, at_x(off, zmate), LPW), lzr.at[j, 2 + d])
        wait(piece(j, f, 0, LPW), lzs.at[j, 0])
        wait(piece(j, f, LPW), lzs.at[j, 1])
        for d in range(3):
            wait(piece(j, f), lxs.at[j, d])
            wait(piece(j, mate, 0, LPW), lxs.at[j, 3 + d])
            wait(piece(j, f, LPW), lzs.at[j, 2 + d])

    def block(st, xoff, h):
        ref = GQ if st == 0 else GP
        slot = at_x(xoff, zmate if st == 2 else zoff)
        return ref.at[slot, HALF * h : HALF * (h + 1), :]

    def send_own(st):
        for h in (0, 1):
            put_same(block(st, 0, h), right, xs.at[st, 0, h], xr.at[st, 0, h])
            put_same(block(st, 0, 1 - h), left, xs.at[st, 1, 1 - h], xr.at[st, 1, 1 - h])

    def to_mate(d, h):
        b = GQ.at[at_x(d, zoff), HALF * h : HALF * (h + 1), :]
        put_same(b, mate, zs.at[d, h], zr.at[d, h])

    def start_q():
        wait(GQ.at[f], p1r.at[0])
        to_mate(0, 0)
        to_mate(0, 1)
        send_own(0)

    def start_p():
        wait(GP.at[f], p1r.at[1])
        put_same(GP.at[f], mate, ps, pr)
        send_own(1)

    def start_mate_p():
        wait(GP.at[mate], pr)
        send_own(2)

    def forward(st, last):
        if not last:
            wait(block(st, 3, 0), xr.at[st, 0, 0])
            put_same(block(st, 3, 0), right, xs.at[st, 2, 0], xr.at[st, 2, 0])
            wait(block(st, 1, 1), xr.at[st, 1, 1])
            put_same(block(st, 1, 1), left, xs.at[st, 2, 1], xr.at[st, 2, 1])
            if st == 0:
                to_mate(3, 0)
                to_mate(1, 1)
        else:
            wait(block(st, 3, 1), xr.at[st, 0, 1])
            wait(block(st, 1, 0), xr.at[st, 1, 0])
            if st == 0:
                to_mate(3, 1)
                to_mate(1, 0)

    def far_in(st):
        for h in (0, 1):
            wait(block(st, 2, h), xr.at[st, 2, h])
            if st == 0:
                to_mate(2, h)

    def mate_q(d):
        for h in (0, 1):
            wait(GQ.at[at_x(d, zmate), HALF * h : HALF * (h + 1), :], zr.at[d, h])

    def count():
        wait(C1, cr.at[0])
        C2[f] = jnp.sum(C1[...], axis=0)
        for d in (1, 2, 3):
            put_same(C2.at[f], at_x(d, zoff), cs.at[1], cr.at[1])
        for d in (0, 1, 2, 3):
            put_same(C2.at[f], at_x(d, zmate), cs.at[1], cr.at[1])

    base = (9 * f) // 2
    half_tile = 64 * lax.rem(f, 2)

    def gram_slot(s):
        for i in range(WIN // 128):
            j = base + i
            dst = slice(128 * i, 128 * (i + 1))

            @pl.when(j < PW // 128)
            def _():
                XT[:, dst] = GP[s, :, pl.ds(pl.multiple_of(128 * j, 128), 128)]

            @pl.when(j >= PW // 128)
            def _():
                XT[:, dst] = GQ[s, :, pl.ds(pl.multiple_of(128 * (j - PW // 128), 128), 128)]

        TT[...] = XT[...].T
        LT[:TILE, :] = TT[pl.ds(pl.multiple_of(half_tile, 64), TILE), :]
        tsum[...] += jnp.dot(LT[:TILE, :], jnp.ones((SLOT, 128), jnp.bfloat16), preferred_element_type=jnp.float32)
        for ref, n, r0 in ((GP, PW, 0), (GQ, QW, PW)):

            def chunk(i, _):
                q = pl.multiple_of(512 * i, 512)
                r = pl.ds(pl.multiple_of(r0 + q, 512), 512)
                acc = jnp.dot(LT[...], ref[s, :, pl.ds(q, 512)], preferred_element_type=jnp.float32)
                gram[:, r] += acc[:TILE]
                ssum[:, r] += acc[TILE:]
                return 0

            lax.fori_loop(0, n // 512, chunk, 0)

    lead_a(0)
    start_q()
    lead_b(0)
    lead_c(0)
    start_p()
    lead_d(0)
    own_copy.wait()

    events = {
        0: [lambda: lead_a(1), lambda: lead_a(2)],
        1: [lambda: lead_b(1), lambda: lead_b(2), start_mate_p],
        2: [lambda: lead_c(1), lambda: lead_c(2), count],
        3: [lambda: forward(0, False)],
        4: [lambda: lead_d(1), lambda: forward(0, True)],
        5: [lambda: lead_d(2), lambda: forward(1, False)],
        6: [lambda: far_in(0)],
        8: [lambda: mate_q(0)],
        9: [lambda: forward(2, False)],
        13: [lambda: forward(1, True)],
    }

    def hooks(k, place):
        for at, evs in events.items():
            if at % 2 == place:

                @pl.when(k == at // 2)
                def _():
                    for ev in evs:
                        ev()

    def step(k, _):
        chol_step(W, k, SA, SM, functools.partial(hooks, k))
        hooks(k, 1)

        @pl.when((k == 1) | (k == 4) | (k >= 7))
        def _():
            gram_slot(jnp.where(k == 1, f, jnp.where(k == 4, mate, jnp.where(k == 7, right, left))))

        return 0

    lax.fori_loop(0, PANEL // NB, step, 0)
    panel[...] = W[PANEL : PANEL + OWN, :]

    far_in(1)
    gram_slot(far)
    forward(2, True)
    mate_q(1)
    gram_slot(at_x(1, zmate))
    mate_q(3)
    gram_slot(at_x(3, zmate))
    far_in(2)
    mate_q(2)
    gram_slot(at_x(2, zmate))

    wait(C2.at[0:7], cr.at[1])
    cnt[...] = jnp.sum(C2[...], axis=0)

    for src, rows in ((0, (432, 96, 0)), (1, (576, 576, 336))):

        @pl.when(f == src)
        def _():
            for j in range(NPAN):
                if rows[j]:
                    wait(prev.at[0 : rows[j], 0:COLS], ls.at[j])

    wait(stq.at[0:15], p1s.at[0])
    wait(stp.at[0:15], p1s.at[1])
    wait(cst.at[0:15], cs.at[0])
    wait(C2.at[0:7], cs.at[1])
    wait(GP.at[f], ps)
    for st in range(3):
        for d in range(3):
            for h in (0, 1):
                wait(block(st, 0, h), xs.at[st, d, h])
    for d in range(4):
        for h in (0, 1):
            wait(GQ.at[f, HALF * h : HALF * (h + 1), :], zs.at[d, h])


def exchange(stp, stq, cst, prev):
    dma = pltpu.SemaphoreType.DMA
    any_space = pl.BlockSpec(memory_space=pl.ANY)
    vmem = pl.BlockSpec(memory_space=pltpu.VMEM)
    return pl.pallas_call(
        kernel,
        out_shape=(
            jax.ShapeDtypeStruct((TILE, D), jnp.float32),
            jax.ShapeDtypeStruct((OWN, PANEL), jnp.float32),
            jax.ShapeDtypeStruct((LHS - TILE, D), jnp.float32),
            jax.ShapeDtypeStruct((TILE, 128), jnp.float32),
            jax.ShapeDtypeStruct((8, 128), jnp.float32),
        ),
        in_specs=[any_space] * 4,
        out_specs=(vmem,) * 5,
        scratch_shapes=[
            pltpu.VMEM((FEAT, SLOT, PW), jnp.bfloat16),
            pltpu.VMEM((FEAT, SLOT, QW), jnp.bfloat16),
            pltpu.VMEM((ROWS, PANEL), jnp.float32),
            pltpu.VMEM((SLOT, WIN), jnp.bfloat16),
            pltpu.VMEM((WIN, SLOT), jnp.bfloat16),
            pltpu.VMEM((LHS, SLOT), jnp.bfloat16),
            pltpu.VMEM((NB, NB), jnp.float32),
            pltpu.VMEM((NB, NB), jnp.float32),
            pltpu.VMEM((CLS, 8, 128), jnp.float32),
            pltpu.VMEM((FEAT, 8, 128), jnp.float32),
            dma((2,)),
            dma((2,)),
            dma((NPAN,)),
            dma((NPAN,)),
            dma((NPAN, 6)),
            dma((NPAN, 6)),
            dma((NPAN, 5)),
            dma((NPAN, 5)),
            dma((3, 3, 2)),
            dma((3, 3, 2)),
            dma((4, 2)),
            dma((4, 2)),
            dma(()),
            dma(()),
            dma((2,)),
            dma((2,)),
            dma(()),
        ],
        compiler_params=pltpu.CompilerParams(
            collective_id=0, has_side_effects=True, vmem_limit_bytes=60 * 2**20
        ),
        cost_estimate=pl.CostEstimate(flops=2 * 2048 * 4608 * 640, bytes_accessed=40 * 2**20, transcendentals=0),
    )(stp, stq, cst, prev)


def body(embeddings, labels, previous):
    rows = embeddings.shape[0]
    label = labels[:, 0]
    onehot = (label[:, None] == jnp.arange(CLS, dtype=jnp.int32)[None, :]).astype(jnp.float32)
    before = (jnp.arange(rows)[:, None] > jnp.arange(rows)[None, :]).astype(jnp.float32)
    rank = jnp.sum(jnp.dot(before, onehot) * onehot, axis=1).astype(jnp.int32)
    place = label * CAP + rank
    pick = (jnp.arange(CLS * CAP, dtype=jnp.int32)[:, None] == place[None, :]).astype(jnp.bfloat16)
    stp = jnp.dot(pick, embeddings[:, :PW]).reshape(CLS, CAP, PW)
    stq = jnp.dot(pick, embeddings[:, PW:]).reshape(CLS, CAP, QW)
    counts = jnp.sum(onehot, axis=0)
    cst = jnp.broadcast_to(counts[:, None, None], (CLS, 8, 128))
    gram, panel, ssum, tsum, cnt = exchange(stp, stq, cst, previous[0])
    total = cnt[0, 0]
    class_cov = (gram / total - (tsum[:, :1] / total) * (ssum[:1, :] / total)).T
    return class_cov[None], panel[None]


def solution(mesh):
    return jax.shard_map(
        body,
        mesh=mesh,
        in_specs=(P(("cls", "feat"), None), P(("cls", "feat"), None), P("cls", "feat", None)),
        out_specs=(P("cls", None, "feat"), P("cls", "feat", None)),
        check_vma=False,
    )
```

```python
import functools

import jax
import jax.numpy as jnp
from jax import lax
from jax.experimental import pallas as pl
from jax.experimental.pallas import tpu as pltpu
from jax.sharding import PartitionSpec as P

MESH = pl.DeviceIdType.MESH
HI = lax.Precision.HIGHEST
D = 4608
CAP = 16
CLS = 16
FEAT = 8
PW = 2560
QW = D - PW
SLOT = CAP * CLS
HALF = SLOT // 2
TILE = D // FEAT
WIN = 640
PANEL = 1152
OWN = 576
ROWS = 1792
NB = 128
COLS = 384
NPAN = 3
PIECE = (144, 96, 48)
LPW = 128
LHS = TILE + 16


def dot_t(a, b):
    return lax.dot_general(a, b, (((1,), (1,)), ((), ())), precision=HI, preferred_element_type=jnp.float32)


def diag_inverse(W, r0, SA, SM):
    SA[...] = W[pl.ds(r0, NB), pl.ds(r0, NB)]
    row = lax.broadcasted_iota(jnp.int32, (NB, NB), 0)
    col = lax.broadcasted_iota(jnp.int32, (NB, NB), 1)
    SM[...] = jnp.where(row == col, 1.0, 0.0).astype(jnp.float32)
    sub = lax.broadcasted_iota(jnp.int32, (8, NB), 0)
    for g in range(NB // 8):
        lo = 8 * g
        pa = SA[lo : lo + 8, :]
        pm = SM[lo : lo + 8, :]
        cols = [jnp.broadcast_to(pa[:, lo + t : lo + t + 1], (8, NB)) for t in range(8)]
        scale = jnp.zeros((8, NB), jnp.float32)
        invs, rows_a, rows_m, heads = [], [], [], []
        for t in range(8):
            heads.append([jnp.broadcast_to(cols[u][t : t + 1, :], (8, NB)) for u in range(8)])
            rows_a.append(jnp.broadcast_to(pa[t : t + 1, :], (8, NB)))
            rows_m.append(jnp.broadcast_to(pm[t : t + 1, :], (8, NB)))
            invs.append(1.0 / heads[t][t])
            m = jnp.where(sub > t, cols[t] * invs[t], 0.0)
            scale = jnp.where(sub == t, heads[t][t], scale)
            for u in range(t + 1, 8):
                cols[u] = cols[u] - m * heads[t][u]
            pa = pa - m * rows_a[t]
            pm = pm - m * rows_m[t]
        SM[lo : lo + 8, :] = pm * lax.rsqrt(scale)
        for i in range(g + 1, NB // 8):
            r = slice(8 * i, 8 * i + 8)
            a = SA[r, :]
            b = SM[r, :]
            q = [jnp.broadcast_to(a[:, lo + t : lo + t + 1], (8, NB)) for t in range(8)]
            for t in range(8):
                m = q[t] * invs[t]
                a = a - m * rows_a[t]
                b = b - m * rows_m[t]
                for u in range(t + 1, 8):
                    q[u] = q[u] - m * heads[t][u]
            SA[r, :] = a
            SM[r, :] = b


def chol_step(W, k, SA, SM, hook):
    r0 = pl.multiple_of(k * NB, NB)
    b = lax.rem(k, 3)
    s = k // 3
    for st in (1, 2):

        @pl.when((b == 0) & (s == st))
        def _():
            c0 = 384 * st

            def body(i, _):
                r = pl.multiple_of(c0 + i * 128, 128)
                acc = W[pl.ds(r, 128), c0 : c0 + 384]
                for q in range(st):
                    acc = acc - dot_t(
                        W[pl.ds(r, 128), 384 * q : 384 * q + 384], W[c0 : c0 + 384, 384 * q : 384 * q + 384]
                    )
                W[pl.ds(r, 128), c0 : c0 + 384] = acc
                return 0

            lax.fori_loop(0, (ROWS - c0) // 128, body, 0)

    diag_inverse(W, r0, SA, SM)
    hook(0)

    def tb(i, _):
        r = pl.multiple_of(i * 256, 256)
        W[pl.ds(r, 256), pl.ds(r0, NB)] = dot_t(W[pl.ds(r, 256), pl.ds(r0, NB)], SM[...])
        return 0

    lax.fori_loop((k + 1) // 2, ROWS // 256, tb, 0)
    for bb in (0, 1):

        @pl.when(b == bb)
        def _():
            n = 256 - 128 * bb

            def ub(i, _):
                r = pl.multiple_of(i * 256, 256)
                c1 = pl.multiple_of(r0 + NB, NB)
                W[pl.ds(r, 256), pl.ds(c1, n)] = W[pl.ds(r, 256), pl.ds(c1, n)] - dot_t(
                    W[pl.ds(r, 256), pl.ds(r0, NB)], W[pl.ds(c1, n), pl.ds(r0, NB)]
                )
                return 0

            lax.fori_loop((k + 1) // 2, ROWS // 256, ub, 0)


def kernel(
    emb, lab, prev,
    gram, panel, ssum, tsum, cnt,
    E, STP, STQ, CST, GP, GQ, W, XT, TT, LT, SA, SM, C1, C2,
    p1r, p1s, lr, ls, lxs, lxr, lzs, lzr, xs, xr, zs, zr, ps, pr, cr, cs, own_sem, emb_sem,
):
    c = lax.axis_index("cls")
    f = lax.axis_index("feat")
    x = lax.rem(f, 4)
    zoff = f - x
    zmate = 4 - zoff
    mate = x + zmate
    zhi = lax.rem(c // 2, 2)

    def at_x(d, z):
        return z + lax.rem(x + d, 4)

    right, left, far = at_x(1, zoff), at_x(3, zoff), at_x(2, zoff)

    bar = pltpu.get_barrier_semaphore()

    def sig(cc, ff):
        pl.semaphore_signal(bar, inc=1, device_id=(cc, ff), device_id_type=MESH)

    def sig_cls(cc, _):
        @pl.when(cc != c)
        def _():
            sig(cc, f)

        sig(cc, mate)
        return 0

    emb_copy = pltpu.make_async_copy(emb, E, emb_sem)
    emb_copy.start()
    own_copy = pltpu.make_async_copy(prev, W.at[PANEL : PANEL + OWN, :], own_sem)
    own_copy.start()
    lax.fori_loop(0, CLS, sig_cls, 0)
    for d in (1, 2, 3):
        sig(c, at_x(d, zoff))
        sig(c, at_x(d, zmate))
    pl.semaphore_wait(bar, 37)

    def put(src, dst, dev, ssem, rsem):
        pltpu.make_async_remote_copy(
            src_ref=src, dst_ref=dst, send_sem=ssem, recv_sem=rsem, device_id=dev, device_id_type=MESH
        ).start()

    def wait(ref, sem):
        pltpu.make_async_copy(ref, ref, sem).wait()

    def put_same(ref, ff, ssem, rsem):
        put(ref, ref, (c, ff), ssem, rsem)

    def piece(j, i, lo=0, hi=COLS):
        r = pl.multiple_of(COLS * j + PIECE[j] * i, 8)
        return W.at[pl.ds(r, PIECE[j]), COLS * j + lo : COLS * j + hi]

    for src in (0, 1):

        @pl.when(f == src)
        def _():
            for j in range(NPAN):
                for i in range(FEAT):
                    r = COLS * j + PIECE[j] * i
                    if r // OWN != src:
                        continue
                    r = r - OWN * src
                    ref = prev.at[r : r + PIECE[j], COLS * j : COLS * (j + 1)]
                    if i == src:
                        pltpu.make_async_copy(ref, piece(j, i), lr.at[j]).start()
                    else:
                        put(ref, piece(j, i), (c, i), ls.at[j], lr.at[j])

    n = emb.shape[0]
    label = lab[...].astype(jnp.float32)
    onehot = (lax.broadcasted_iota(jnp.int32, (CLS, n), 0).astype(jnp.float32) == label).astype(jnp.float32)
    t0 = lax.broadcasted_iota(jnp.int32, (n, n), 0)
    t1 = lax.broadcasted_iota(jnp.int32, (n, n), 1)
    ahead = jnp.dot(
        onehot.astype(jnp.bfloat16), (t0 < t1).astype(jnp.float32).astype(jnp.bfloat16), preferred_element_type=jnp.float32
    )
    place = label * CAP + jnp.sum(ahead * onehot, axis=0, keepdims=True)
    pick = (lax.broadcasted_iota(jnp.int32, (SLOT, n), 0).astype(jnp.float32) == place).astype(jnp.float32)
    pick = pick.astype(jnp.bfloat16)
    counts = jnp.sum(onehot, axis=1, keepdims=True)
    for i in range(CLS):
        CST[i] = jnp.broadcast_to(counts[i : i + 1, :], (8, 128))
    emb_copy.wait()
    for ref, w, c0 in ((STQ, QW, PW), (STP, PW, 0)):
        for i in range(w // 512):
            cols = slice(512 * i, 512 * (i + 1))
            chosen = jnp.dot(pick, E[:, c0 + 512 * i : c0 + 512 * (i + 1)], preferred_element_type=jnp.float32)
            ref[:, cols] = chosen.astype(jnp.bfloat16)

    def rows_of(ref, cc):
        return ref.at[pl.ds(pl.multiple_of(CAP * cc, CAP), CAP), :]

    def route(cc, _):
        same = lax.rem(cc // 2, 2) == zhi
        g = jnp.where(same, f, mate)
        r = pl.multiple_of(CAP * c, CAP)
        dq = GQ.at[g, pl.ds(r, CAP), :]

        @pl.when(cc == c)
        def _():
            pltpu.make_async_copy(rows_of(STQ, cc), dq, p1r.at[0]).start()
            pltpu.make_async_copy(CST.at[cc], C1.at[c], cr.at[0]).start()

        @pl.when(cc != c)
        def _():
            put(rows_of(STQ, cc), dq, (cc, g), p1s.at[0], p1r.at[0])
            put(CST.at[cc], C1.at[c], (cc, f), cs.at[0], cr.at[0])

        return 0

    lax.fori_loop(0, CLS, route, 0)

    def route_p(cc, _):
        same = lax.rem(cc // 2, 2) == zhi
        g = jnp.where(same, f, mate)
        r = pl.multiple_of(CAP * c, CAP)
        dp = GP.at[g, pl.ds(r, CAP), :]

        @pl.when(cc == c)
        def _():
            pltpu.make_async_copy(rows_of(STP, cc), dp, p1r.at[1]).start()

        @pl.when(cc != c)
        def _():
            put(rows_of(STP, cc), dp, (cc, g), p1s.at[1], p1r.at[1])

        return 0


    def zero(i, _):
        gram[:, pl.ds(pl.multiple_of(512 * i, 512), 512)] = jnp.zeros((TILE, 512), jnp.float32)
        return 0

    lax.fori_loop(0, D // 512, zero, 0)
    ssum[...] = jnp.zeros_like(ssum)
    tsum[...] = jnp.zeros_like(tsum)
    LT[TILE:, :] = jnp.ones((LHS - TILE, SLOT), jnp.bfloat16)
    W[PANEL + OWN :, :] = jnp.zeros((ROWS - PANEL - OWN, PANEL), jnp.float32)

    along_x = ((0, right), (1, left), (2, far))
    from_x = ((0, 3), (1, 1), (2, 2))

    def lead_a(j):
        wait(piece(j, f), lr.at[j])
        put_same(piece(j, f, 0, LPW), mate, lzs.at[j, 0], lzr.at[j, 0])
        for d, ff in along_x:
            put_same(piece(j, f), ff, lxs.at[j, d], lxr.at[j, d])
        put_same(piece(j, f, LPW), mate, lzs.at[j, 1], lzr.at[j, 1])

    def lead_b(j):
        wait(piece(j, mate, 0, LPW), lzr.at[j, 0])
        for d, ff in along_x:
            put_same(piece(j, mate, 0, LPW), ff, lxs.at[j, 3 + d], lxr.at[j, 3 + d])

    def lead_c(j):
        for d, off in from_x:
            wait(piece(j, at_x(off, zoff)), lxr.at[j, d])
            put_same(piece(j, at_x(off, zoff), LPW), mate, lzs.at[j, 2 + d], lzr.at[j, 2 + d])

    def lead_d(j):
        wait(piece(j, mate, LPW), lzr.at[j, 1])
        for d, off in from_x:
            wait(piece(j, at_x(off, zmate), 0, LPW), lxr.at[j, 3 + d])
            wait(piece(j, at_x(off, zmate), LPW), lzr.at[j, 2 + d])
        wait(piece(j, f, 0, LPW), lzs.at[j, 0])
        wait(piece(j, f, LPW), lzs.at[j, 1])
        for d in range(3):
            wait(piece(j, f), lxs.at[j, d])
            wait(piece(j, mate, 0, LPW), lxs.at[j, 3 + d])
            wait(piece(j, f, LPW), lzs.at[j, 2 + d])

    def block(st, xoff, h):
        ref = GQ if st == 0 else GP
        slot = at_x(xoff, zmate if st == 2 else zoff)
        return ref.at[slot, HALF * h : HALF * (h + 1), :]

    def send_own(st):
        for h in (0, 1):
            put_same(block(st, 0, h), right, xs.at[st, 0, h], xr.at[st, 0, h])
            put_same(block(st, 0, 1 - h), left, xs.at[st, 1, 1 - h], xr.at[st, 1, 1 - h])

    def to_mate(d, h):
        b = GQ.at[at_x(d, zoff), HALF * h : HALF * (h + 1), :]
        put_same(b, mate, zs.at[d, h], zr.at[d, h])

    def start_q():
        wait(GQ.at[f], p1r.at[0])
        lax.fori_loop(0, CLS, route_p, 0)
        to_mate(0, 0)
        to_mate(0, 1)
        send_own(0)

    def start_p():
        wait(GP.at[f], p1r.at[1])
        put_same(GP.at[f], mate, ps, pr)
        send_own(1)

    def start_mate_p():
        wait(GP.at[mate], pr)
        send_own(2)

    def forward(st, last):
        if not last:
            wait(block(st, 3, 0), xr.at[st, 0, 0])
            put_same(block(st, 3, 0), right, xs.at[st, 2, 0], xr.at[st, 2, 0])
            wait(block(st, 1, 1), xr.at[st, 1, 1])
            put_same(block(st, 1, 1), left, xs.at[st, 2, 1], xr.at[st, 2, 1])
            if st == 0:
                to_mate(3, 0)
                to_mate(1, 1)
        else:
            wait(block(st, 3, 1), xr.at[st, 0, 1])
            wait(block(st, 1, 0), xr.at[st, 1, 0])
            if st == 0:
                to_mate(3, 1)
                to_mate(1, 0)

    def far_in(st):
        for h in (0, 1):
            wait(block(st, 2, h), xr.at[st, 2, h])
            if st == 0:
                to_mate(2, h)

    def mate_q(d):
        for h in (0, 1):
            wait(GQ.at[at_x(d, zmate), HALF * h : HALF * (h + 1), :], zr.at[d, h])

    def count():
        wait(C1, cr.at[0])
        C2[f] = jnp.sum(C1[...], axis=0)
        for d in (1, 2, 3):
            put_same(C2.at[f], at_x(d, zoff), cs.at[1], cr.at[1])
        for d in (0, 1, 2, 3):
            put_same(C2.at[f], at_x(d, zmate), cs.at[1], cr.at[1])

    base = (9 * f) // 2
    half_tile = 64 * lax.rem(f, 2)

    def gram_slot(s):
        for i in range(WIN // 128):
            j = base + i
            dst = slice(128 * i, 128 * (i + 1))

            @pl.when(j < PW // 128)
            def _():
                XT[:, dst] = GP[s, :, pl.ds(pl.multiple_of(128 * j, 128), 128)]

            @pl.when(j >= PW // 128)
            def _():
                XT[:, dst] = GQ[s, :, pl.ds(pl.multiple_of(128 * (j - PW // 128), 128), 128)]

        TT[...] = XT[...].T
        LT[:TILE, :] = TT[pl.ds(pl.multiple_of(half_tile, 64), TILE), :]
        tsum[...] += jnp.dot(LT[:TILE, :], jnp.ones((SLOT, 128), jnp.bfloat16), preferred_element_type=jnp.float32)
        for ref, n, r0 in ((GP, PW, 0), (GQ, QW, PW)):

            def chunk(i, _):
                q = pl.multiple_of(512 * i, 512)
                r = pl.ds(pl.multiple_of(r0 + q, 512), 512)
                acc = jnp.dot(LT[...], ref[s, :, pl.ds(q, 512)], preferred_element_type=jnp.float32)
                gram[:, r] += acc[:TILE]
                ssum[:, r] += acc[TILE:]
                return 0

            lax.fori_loop(0, n // 512, chunk, 0)

    lead_a(0)
    lead_b(0)
    start_q()
    lead_c(0)
    lead_a(1)
    lead_a(2)
    lead_d(0)
    own_copy.wait()

    events = {
        0: [start_p],
        1: [lambda: lead_b(1), lambda: lead_b(2)],
        2: [lambda: lead_c(1), lambda: lead_c(2), count],
        3: [lambda: forward(0, False)],
        4: [lambda: lead_d(1), lambda: forward(0, True)],
        5: [lambda: lead_d(2)],
        8: [lambda: far_in(0)],
        9: [lambda: mate_q(0), start_mate_p],
        13: [lambda: forward(1, False)],
        15: [lambda: forward(1, True)],
    }

    def hooks(k, place):
        for at, evs in events.items():
            if at % 2 == place:

                @pl.when(k == at // 2)
                def _():
                    for ev in evs:
                        ev()

    def step(k, _):
        chol_step(W, k, SA, SM, functools.partial(hooks, k))
        hooks(k, 1)

        @pl.when((k == 1) | (k == 5) | (k >= 7))
        def _():
            gram_slot(jnp.where(k == 1, f, jnp.where(k == 5, mate, jnp.where(k == 7, right, left))))

        return 0

    lax.fori_loop(0, PANEL // NB, step, 0)
    panel[...] = W[PANEL : PANEL + OWN, :]

    forward(2, False)
    far_in(1)
    gram_slot(far)
    forward(2, True)
    mate_q(1)
    gram_slot(at_x(1, zmate))
    mate_q(3)
    gram_slot(at_x(3, zmate))
    far_in(2)
    mate_q(2)
    gram_slot(at_x(2, zmate))

    wait(C2.at[0:7], cr.at[1])
    cnt[...] = jnp.sum(C2[...], axis=0)

    for src, rows in ((0, (432, 96, 0)), (1, (576, 576, 336))):

        @pl.when(f == src)
        def _():
            for j in range(NPAN):
                if rows[j]:
                    wait(prev.at[0 : rows[j], 0:COLS], ls.at[j])

    wait(STQ.at[0 : 15 * CAP, :], p1s.at[0])
    wait(STP.at[0 : 15 * CAP, :], p1s.at[1])
    wait(CST.at[0:15], cs.at[0])
    wait(C2.at[0:7], cs.at[1])
    wait(GP.at[f], ps)
    for st in range(3):
        for d in range(3):
            for h in (0, 1):
                wait(block(st, 0, h), xs.at[st, d, h])
    for d in range(4):
        for h in (0, 1):
            wait(GQ.at[f, HALF * h : HALF * (h + 1), :], zs.at[d, h])


def exchange(emb, lab, prev):
    dma = pltpu.SemaphoreType.DMA
    any_space = pl.BlockSpec(memory_space=pl.ANY)
    vmem = pl.BlockSpec(memory_space=pltpu.VMEM)
    return pl.pallas_call(
        kernel,
        out_shape=(
            jax.ShapeDtypeStruct((TILE, D), jnp.float32),
            jax.ShapeDtypeStruct((OWN, PANEL), jnp.float32),
            jax.ShapeDtypeStruct((LHS - TILE, D), jnp.float32),
            jax.ShapeDtypeStruct((TILE, 128), jnp.float32),
            jax.ShapeDtypeStruct((8, 128), jnp.float32),
        ),
        in_specs=[any_space, vmem, any_space],
        out_specs=(vmem,) * 5,
        scratch_shapes=[
            pltpu.VMEM((128, D), jnp.bfloat16),
            pltpu.VMEM((SLOT, PW), jnp.bfloat16),
            pltpu.VMEM((SLOT, QW), jnp.bfloat16),
            pltpu.VMEM((CLS, 8, 128), jnp.float32),
            pltpu.VMEM((FEAT, SLOT, PW), jnp.bfloat16),
            pltpu.VMEM((FEAT, SLOT, QW), jnp.bfloat16),
            pltpu.VMEM((ROWS, PANEL), jnp.float32),
            pltpu.VMEM((SLOT, WIN), jnp.bfloat16),
            pltpu.VMEM((WIN, SLOT), jnp.bfloat16),
            pltpu.VMEM((LHS, SLOT), jnp.bfloat16),
            pltpu.VMEM((NB, NB), jnp.float32),
            pltpu.VMEM((NB, NB), jnp.float32),
            pltpu.VMEM((CLS, 8, 128), jnp.float32),
            pltpu.VMEM((FEAT, 8, 128), jnp.float32),
            dma((2,)),
            dma((2,)),
            dma((NPAN,)),
            dma((NPAN,)),
            dma((NPAN, 6)),
            dma((NPAN, 6)),
            dma((NPAN, 5)),
            dma((NPAN, 5)),
            dma((3, 3, 2)),
            dma((3, 3, 2)),
            dma((4, 2)),
            dma((4, 2)),
            dma(()),
            dma(()),
            dma((2,)),
            dma((2,)),
            dma(()),
            dma(()),
        ],
        compiler_params=pltpu.CompilerParams(
            collective_id=0, has_side_effects=True, vmem_limit_bytes=60 * 2**20
        ),
        cost_estimate=pl.CostEstimate(flops=2 * 2048 * 4608 * 640, bytes_accessed=40 * 2**20, transcendentals=0),
    )(emb, lab, prev)


def finish_kernel(gram, ssum, tsum, cnt, out):
    inv = 1.0 / cnt[0:1, 0:1]
    out[...] = gram[...] * inv - (tsum[:, 0:1] * inv) * (ssum[0:1, :] * inv)


def finish(gram, ssum, tsum, cnt):
    h = 64
    return pl.pallas_call(
        finish_kernel,
        grid=(TILE // h,),
        out_shape=jax.ShapeDtypeStruct((TILE, D), jnp.float32),
        in_specs=[
            pl.BlockSpec((h, D), lambda i: (i, 0)),
            pl.BlockSpec((LHS - TILE, D), lambda i: (0, 0)),
            pl.BlockSpec((h, 128), lambda i: (i, 0)),
            pl.BlockSpec((8, 128), lambda i: (0, 0)),
        ],
        out_specs=pl.BlockSpec((h, D), lambda i: (i, 0)),
        compiler_params=pltpu.CompilerParams(vmem_limit_bytes=60 * 2**20),
    )(gram, ssum, tsum, cnt)


def body(embeddings, labels, previous):
    gram, panel, ssum, tsum, cnt = exchange(embeddings, labels.reshape(1, -1), previous[0])
    return finish(gram, ssum, tsum, cnt).T[None], panel[None]


def solution(mesh):
    return jax.shard_map(
        body,
        mesh=mesh,
        in_specs=(P(("cls", "feat"), None), P(("cls", "feat"), None), P("cls", "feat", None)),
        out_specs=(P("cls", None, "feat"), P("cls", "feat", None)),
        check_vma=False,
    )
```

```python
import functools

import jax
import jax.numpy as jnp
from jax import lax
from jax.experimental import pallas as pl
from jax.experimental.pallas import tpu as pltpu
from jax.sharding import PartitionSpec as P

MESH = pl.DeviceIdType.MESH
HI = lax.Precision.HIGHEST
D = 4608
CAP = 16
CLS = 16
FEAT = 8
PW = 2560
QW = D - PW
SLOT = CAP * CLS
HALF = SLOT // 2
TILE = D // FEAT
WIN = 640
PANEL = 1152
OWN = 576
ROWS = 1792
NB = 128
COLS = 384
NPAN = 3
PIECE = (144, 96, 48)
LPW = 128
LHS = TILE + 16


def dot_t(a, b):
    return lax.dot_general(a, b, (((1,), (1,)), ((), ())), precision=HI, preferred_element_type=jnp.float32)


def diag_inverse(W, r0, SA, SM):
    SA[...] = W[pl.ds(r0, NB), pl.ds(r0, NB)]
    row = lax.broadcasted_iota(jnp.int32, (NB, NB), 0)
    col = lax.broadcasted_iota(jnp.int32, (NB, NB), 1)
    SM[...] = jnp.where(row == col, 1.0, 0.0).astype(jnp.float32)
    sub = lax.broadcasted_iota(jnp.int32, (8, NB), 0)
    for g in range(NB // 8):
        lo = 8 * g
        pa = SA[lo : lo + 8, :]
        pm = SM[lo : lo + 8, :]
        cols = [jnp.broadcast_to(pa[:, lo + t : lo + t + 1], (8, NB)) for t in range(8)]
        scale = jnp.zeros((8, NB), jnp.float32)
        invs, rows_a, rows_m, heads = [], [], [], []
        for t in range(8):
            heads.append([jnp.broadcast_to(cols[u][t : t + 1, :], (8, NB)) for u in range(8)])
            rows_a.append(jnp.broadcast_to(pa[t : t + 1, :], (8, NB)))
            rows_m.append(jnp.broadcast_to(pm[t : t + 1, :], (8, NB)))
            invs.append(1.0 / heads[t][t])
            m = jnp.where(sub > t, cols[t] * invs[t], 0.0)
            scale = jnp.where(sub == t, heads[t][t], scale)
            for u in range(t + 1, 8):
                cols[u] = cols[u] - m * heads[t][u]
            pa = pa - m * rows_a[t]
            pm = pm - m * rows_m[t]
        SM[lo : lo + 8, :] = pm * lax.rsqrt(scale)
        for i in range(g + 1, NB // 8):
            r = slice(8 * i, 8 * i + 8)
            a = SA[r, :]
            b = SM[r, :]
            q = [jnp.broadcast_to(a[:, lo + t : lo + t + 1], (8, NB)) for t in range(8)]
            for t in range(8):
                m = q[t] * invs[t]
                a = a - m * rows_a[t]
                b = b - m * rows_m[t]
                for u in range(t + 1, 8):
                    q[u] = q[u] - m * heads[t][u]
            SA[r, :] = a
            SM[r, :] = b


def chol_step(W, k, SA, SM, hook):
    r0 = pl.multiple_of(k * NB, NB)
    b = lax.rem(k, 3)
    s = k // 3
    for st in (1, 2):

        @pl.when((b == 0) & (s == st))
        def _():
            c0 = 384 * st

            def body(i, _):
                r = pl.multiple_of(c0 + i * 128, 128)
                acc = W[pl.ds(r, 128), c0 : c0 + 384]
                for q in range(st):
                    acc = acc - dot_t(
                        W[pl.ds(r, 128), 384 * q : 384 * q + 384], W[c0 : c0 + 384, 384 * q : 384 * q + 384]
                    )
                W[pl.ds(r, 128), c0 : c0 + 384] = acc
                return 0

            lax.fori_loop(0, (ROWS - c0) // 128, body, 0)

    diag_inverse(W, r0, SA, SM)
    hook(0)

    def tb(i, _):
        r = pl.multiple_of(i * 256, 256)
        W[pl.ds(r, 256), pl.ds(r0, NB)] = dot_t(W[pl.ds(r, 256), pl.ds(r0, NB)], SM[...])
        return 0

    lax.fori_loop((k + 1) // 2, ROWS // 256, tb, 0)
    for bb in (0, 1):

        @pl.when(b == bb)
        def _():
            n = 256 - 128 * bb

            def ub(i, _):
                r = pl.multiple_of(i * 256, 256)
                c1 = pl.multiple_of(r0 + NB, NB)
                W[pl.ds(r, 256), pl.ds(c1, n)] = W[pl.ds(r, 256), pl.ds(c1, n)] - dot_t(
                    W[pl.ds(r, 256), pl.ds(r0, NB)], W[pl.ds(c1, n), pl.ds(r0, NB)]
                )
                return 0

            lax.fori_loop((k + 1) // 2, ROWS // 256, ub, 0)


def kernel(
    emb, lab, prev,
    gram, panel, ssum, tsum, cnt,
    E, STP, STQ, CST, GP, GQ, W, XT, TT, LT, SA, SM, C1, C2,
    p1r, p1s, lr, ls, lxs, lxr, lzs, lzr, xs, xr, zs, zr, ps, pr, cr, cs, own_sem, emb_sem,
):
    c = lax.axis_index("cls")
    f = lax.axis_index("feat")
    x = lax.rem(f, 4)
    zoff = f - x
    zmate = 4 - zoff
    mate = x + zmate
    zhi = lax.rem(c // 2, 2)

    def at_x(d, z):
        return z + lax.rem(x + d, 4)

    right, left, far = at_x(1, zoff), at_x(3, zoff), at_x(2, zoff)

    bar = pltpu.get_barrier_semaphore()

    def sig(cc, ff):
        pl.semaphore_signal(bar, inc=1, device_id=(cc, ff), device_id_type=MESH)

    def sig_cls(cc, _):
        @pl.when(cc != c)
        def _():
            sig(cc, f)

        sig(cc, mate)
        return 0

    emb_copy = pltpu.make_async_copy(emb, E, emb_sem)
    emb_copy.start()
    own_copy = pltpu.make_async_copy(prev, W.at[PANEL : PANEL + OWN, :], own_sem)
    own_copy.start()
    lax.fori_loop(0, CLS, sig_cls, 0)
    for d in (1, 2, 3):
        sig(c, at_x(d, zoff))
        sig(c, at_x(d, zmate))
    pl.semaphore_wait(bar, 37)

    def put(src, dst, dev, ssem, rsem):
        pltpu.make_async_remote_copy(
            src_ref=src, dst_ref=dst, send_sem=ssem, recv_sem=rsem, device_id=dev, device_id_type=MESH
        ).start()

    def wait(ref, sem):
        pltpu.make_async_copy(ref, ref, sem).wait()

    def put_same(ref, ff, ssem, rsem):
        put(ref, ref, (c, ff), ssem, rsem)

    def piece(j, i, lo=0, hi=COLS):
        r = pl.multiple_of(COLS * j + PIECE[j] * i, 8)
        return W.at[pl.ds(r, PIECE[j]), COLS * j + lo : COLS * j + hi]

    for src in (0, 1):

        @pl.when(f == src)
        def _():
            for j in range(NPAN):
                for i in range(FEAT):
                    r = COLS * j + PIECE[j] * i
                    if r // OWN != src:
                        continue
                    r = r - OWN * src
                    ref = prev.at[r : r + PIECE[j], COLS * j : COLS * (j + 1)]
                    if i == src:
                        pltpu.make_async_copy(ref, piece(j, i), lr.at[j]).start()
                    else:
                        put(ref, piece(j, i), (c, i), ls.at[j], lr.at[j])

    n = emb.shape[0]
    label = lab[...].astype(jnp.float32)
    onehot = (lax.broadcasted_iota(jnp.int32, (CLS, n), 0).astype(jnp.float32) == label).astype(jnp.float32)
    t0 = lax.broadcasted_iota(jnp.int32, (n, n), 0)
    t1 = lax.broadcasted_iota(jnp.int32, (n, n), 1)
    ahead = jnp.dot(
        onehot.astype(jnp.bfloat16), (t0 < t1).astype(jnp.float32).astype(jnp.bfloat16), preferred_element_type=jnp.float32
    )
    place = label * CAP + jnp.sum(ahead * onehot, axis=0, keepdims=True)
    pick = (lax.broadcasted_iota(jnp.int32, (SLOT, n), 0).astype(jnp.float32) == place).astype(jnp.float32)
    pick = pick.astype(jnp.bfloat16)
    counts = jnp.sum(onehot, axis=1, keepdims=True)
    for i in range(CLS):
        CST[i] = jnp.broadcast_to(counts[i : i + 1, :], (8, 128))
    emb_copy.wait()
    for ref, w, c0 in ((STQ, QW, PW), (STP, PW, 0)):
        for i in range(w // 512):
            cols = slice(512 * i, 512 * (i + 1))
            chosen = jnp.dot(pick, E[:, c0 + 512 * i : c0 + 512 * (i + 1)], preferred_element_type=jnp.float32)
            ref[:, cols] = chosen.astype(jnp.bfloat16)

    def rows_of(ref, cc):
        return ref.at[pl.ds(pl.multiple_of(CAP * cc, CAP), CAP), :]

    def route(cc, _):
        same = lax.rem(cc // 2, 2) == zhi
        g = jnp.where(same, f, mate)
        r = pl.multiple_of(CAP * c, CAP)
        dq = GQ.at[g, pl.ds(r, CAP), :]

        @pl.when(cc == c)
        def _():
            pltpu.make_async_copy(rows_of(STQ, cc), dq, p1r.at[0]).start()
            pltpu.make_async_copy(CST.at[cc], C1.at[c], cr.at[0]).start()

        @pl.when(cc != c)
        def _():
            put(rows_of(STQ, cc), dq, (cc, g), p1s.at[0], p1r.at[0])
            put(CST.at[cc], C1.at[c], (cc, f), cs.at[0], cr.at[0])

        return 0

    lax.fori_loop(0, CLS, route, 0)

    def route_p(cc, _):
        same = lax.rem(cc // 2, 2) == zhi
        g = jnp.where(same, f, mate)
        r = pl.multiple_of(CAP * c, CAP)
        dp = GP.at[g, pl.ds(r, CAP), :]

        @pl.when(cc == c)
        def _():
            pltpu.make_async_copy(rows_of(STP, cc), dp, p1r.at[1]).start()

        @pl.when(cc != c)
        def _():
            put(rows_of(STP, cc), dp, (cc, g), p1s.at[1], p1r.at[1])

        return 0


    def zero(i, _):
        gram[:, pl.ds(pl.multiple_of(512 * i, 512), 512)] = jnp.zeros((TILE, 512), jnp.float32)
        return 0

    lax.fori_loop(0, D // 512, zero, 0)
    ssum[...] = jnp.zeros_like(ssum)
    tsum[...] = jnp.zeros_like(tsum)
    LT[TILE:, :] = jnp.ones((LHS - TILE, SLOT), jnp.bfloat16)
    W[PANEL + OWN :, :] = jnp.zeros((ROWS - PANEL - OWN, PANEL), jnp.float32)

    along_x = ((0, right), (1, left), (2, far))
    from_x = ((0, 3), (1, 1), (2, 2))

    def lead_a(j):
        wait(piece(j, f), lr.at[j])
        put_same(piece(j, f, 0, LPW), mate, lzs.at[j, 0], lzr.at[j, 0])
        for d, ff in along_x:
            put_same(piece(j, f), ff, lxs.at[j, d], lxr.at[j, d])
        put_same(piece(j, f, LPW), mate, lzs.at[j, 1], lzr.at[j, 1])

    def lead_b(j):
        wait(piece(j, mate, 0, LPW), lzr.at[j, 0])
        for d, ff in along_x:
            put_same(piece(j, mate, 0, LPW), ff, lxs.at[j, 3 + d], lxr.at[j, 3 + d])

    def lead_c(j):
        for d, off in from_x:
            wait(piece(j, at_x(off, zoff)), lxr.at[j, d])
            put_same(piece(j, at_x(off, zoff), LPW), mate, lzs.at[j, 2 + d], lzr.at[j, 2 + d])

    def lead_d(j):
        wait(piece(j, mate, LPW), lzr.at[j, 1])
        for d, off in from_x:
            wait(piece(j, at_x(off, zmate), 0, LPW), lxr.at[j, 3 + d])
            wait(piece(j, at_x(off, zmate), LPW), lzr.at[j, 2 + d])
        wait(piece(j, f, 0, LPW), lzs.at[j, 0])
        wait(piece(j, f, LPW), lzs.at[j, 1])
        for d in range(3):
            wait(piece(j, f), lxs.at[j, d])
            wait(piece(j, mate, 0, LPW), lxs.at[j, 3 + d])
            wait(piece(j, f, LPW), lzs.at[j, 2 + d])

    def block(st, xoff, h):
        ref = GQ if st == 0 else GP
        slot = at_x(xoff, zmate if st == 2 else zoff)
        return ref.at[slot, HALF * h : HALF * (h + 1), :]

    def send_own(st):
        for h in (0, 1):
            put_same(block(st, 0, h), right, xs.at[st, 0, h], xr.at[st, 0, h])
            put_same(block(st, 0, 1 - h), left, xs.at[st, 1, 1 - h], xr.at[st, 1, 1 - h])

    def to_mate(d, h):
        b = GQ.at[at_x(d, zoff), HALF * h : HALF * (h + 1), :]
        put_same(b, mate, zs.at[d, h], zr.at[d, h])

    def start_q():
        wait(GQ.at[f], p1r.at[0])
        lax.fori_loop(0, CLS, route_p, 0)
        to_mate(0, 0)
        to_mate(0, 1)
        send_own(0)

    def start_p():
        wait(GP.at[f], p1r.at[1])
        for h in (0, 1):
            put_same(block(1, 0, h), mate, ps.at[h], pr.at[h])
        send_own(1)

    def start_mate_p():
        for h in (0, 1):
            wait(block(2, 0, h), pr.at[h])
            put_same(block(2, 0, h), right if h == 0 else left, xs.at[2, h, h], xr.at[2, h, h])
        for h in (0, 1):
            put_same(block(2, 0, h), left if h == 0 else right, xs.at[2, 1 - h, h], xr.at[2, 1 - h, h])

    def forward(st, last):
        if not last:
            wait(block(st, 3, 0), xr.at[st, 0, 0])
            put_same(block(st, 3, 0), right, xs.at[st, 2, 0], xr.at[st, 2, 0])
            wait(block(st, 1, 1), xr.at[st, 1, 1])
            put_same(block(st, 1, 1), left, xs.at[st, 2, 1], xr.at[st, 2, 1])
            if st == 0:
                to_mate(3, 0)
                to_mate(1, 1)
        else:
            wait(block(st, 3, 1), xr.at[st, 0, 1])
            wait(block(st, 1, 0), xr.at[st, 1, 0])
            if st == 0:
                to_mate(3, 1)
                to_mate(1, 0)

    def far_in(st):
        for h in (0, 1):
            wait(block(st, 2, h), xr.at[st, 2, h])
            if st == 0:
                to_mate(2, h)

    def mate_q(d):
        for h in (0, 1):
            wait(GQ.at[at_x(d, zmate), HALF * h : HALF * (h + 1), :], zr.at[d, h])

    def count():
        wait(C1, cr.at[0])
        C2[f] = jnp.sum(C1[...], axis=0)
        for d in (1, 2, 3):
            put_same(C2.at[f], at_x(d, zoff), cs.at[1], cr.at[1])
        for d in (0, 1, 2, 3):
            put_same(C2.at[f], at_x(d, zmate), cs.at[1], cr.at[1])

    base = (9 * f) // 2
    half_tile = 64 * lax.rem(f, 2)

    def gram_slot(s):
        for i in range(WIN // 128):
            j = base + i
            dst = slice(128 * i, 128 * (i + 1))

            @pl.when(j < PW // 128)
            def _():
                XT[:, dst] = GP[s, :, pl.ds(pl.multiple_of(128 * j, 128), 128)]

            @pl.when(j >= PW // 128)
            def _():
                XT[:, dst] = GQ[s, :, pl.ds(pl.multiple_of(128 * (j - PW // 128), 128), 128)]

        TT[...] = XT[...].T
        LT[:TILE, :] = TT[pl.ds(pl.multiple_of(half_tile, 64), TILE), :]
        tsum[...] += jnp.dot(LT[:TILE, :], jnp.ones((SLOT, 128), jnp.bfloat16), preferred_element_type=jnp.float32)
        for ref, n, r0 in ((GP, PW, 0), (GQ, QW, PW)):

            def chunk(i, _):
                q = 512 * i
                r = pl.ds(r0 + q, 512)
                acc = jnp.dot(LT[...], ref[s, :, pl.ds(q, 512)], preferred_element_type=jnp.float32)
                gram[:, r] += acc[:TILE]
                ssum[:, r] += acc[TILE:]
                return 0

            for i in range(n // 512):
                chunk(i, 0)

    lead_a(0)
    lead_b(0)
    start_q()
    lead_c(0)
    lead_a(1)
    lead_a(2)
    lead_d(0)
    own_copy.wait()

    events = {
        0: [start_p],
        1: [lambda: lead_b(1), lambda: lead_b(2)],
        2: [lambda: lead_c(1), lambda: lead_c(2), count],
        4: [lambda: lead_d(1), lambda: forward(0, False)],
        5: [lambda: lead_d(2), lambda: forward(0, True)],
        7: [start_mate_p],
        8: [lambda: far_in(0)],
        11: [lambda: mate_q(0)],
        12: [lambda: forward(1, False)],
        14: [lambda: forward(1, True)],
        16: [lambda: forward(2, False)],
    }

    def hooks(k, place):
        for at, evs in events.items():
            if at % 2 == place:

                @pl.when(k == at // 2)
                def _():
                    for ev in evs:
                        ev()

    def step(k, _):
        chol_step(W, k, SA, SM, functools.partial(hooks, k))
        hooks(k, 1)

        @pl.when((k == 1) | (k == 6) | (k >= 7))
        def _():
            gram_slot(jnp.where(k == 1, f, jnp.where(k == 6, mate, jnp.where(k == 7, right, left))))

        return 0

    lax.fori_loop(0, PANEL // NB, step, 0)
    panel[...] = W[PANEL : PANEL + OWN, :]

    far_in(1)

    def last(n, _):
        @pl.when(n == 1)
        def _():
            forward(2, True)
            mate_q(1)

        @pl.when(n == 2)
        def _():
            mate_q(3)

        @pl.when(n == 3)
        def _():
            far_in(2)
            mate_q(2)

        d = jnp.where(n == 1, 1, jnp.where(n == 2, 3, 2))
        gram_slot(at_x(d, jnp.where(n == 0, zoff, zmate)))
        return 0

    lax.fori_loop(0, 4, last, 0)

    wait(C2.at[0:7], cr.at[1])
    cnt[...] = jnp.sum(C2[...], axis=0)

    for src, rows in ((0, (432, 96, 0)), (1, (576, 576, 336))):

        @pl.when(f == src)
        def _():
            for j in range(NPAN):
                if rows[j]:
                    wait(prev.at[0 : rows[j], 0:COLS], ls.at[j])

    wait(STQ.at[0 : 15 * CAP, :], p1s.at[0])
    wait(STP.at[0 : 15 * CAP, :], p1s.at[1])
    wait(CST.at[0:15], cs.at[0])
    wait(C2.at[0:7], cs.at[1])
    for h in (0, 1):
        wait(block(1, 0, h), ps.at[h])
    for st in range(3):
        for d in range(3):
            for h in (0, 1):
                wait(block(st, 0, h), xs.at[st, d, h])
    for d in range(4):
        for h in (0, 1):
            wait(GQ.at[f, HALF * h : HALF * (h + 1), :], zs.at[d, h])


def exchange(emb, lab, prev):
    dma = pltpu.SemaphoreType.DMA
    any_space = pl.BlockSpec(memory_space=pl.ANY)
    vmem = pl.BlockSpec(memory_space=pltpu.VMEM)
    return pl.pallas_call(
        kernel,
        out_shape=(
            pltpu.VMEM((TILE, D), jnp.float32),
            pltpu.VMEM((OWN, PANEL), jnp.float32),
            pltpu.VMEM((LHS - TILE, D), jnp.float32),
            pltpu.VMEM((TILE, 128), jnp.float32),
            pltpu.VMEM((8, 128), jnp.float32),
        ),
        in_specs=[any_space, vmem, any_space],
        out_specs=(vmem,) * 5,
        scratch_shapes=[
            pltpu.VMEM((128, D), jnp.bfloat16),
            pltpu.VMEM((SLOT, PW), jnp.bfloat16),
            pltpu.VMEM((SLOT, QW), jnp.bfloat16),
            pltpu.VMEM((CLS, 8, 128), jnp.float32),
            pltpu.VMEM((FEAT, SLOT, PW), jnp.bfloat16),
            pltpu.VMEM((FEAT, SLOT, QW), jnp.bfloat16),
            pltpu.VMEM((ROWS, PANEL), jnp.float32),
            pltpu.VMEM((SLOT, WIN), jnp.bfloat16),
            pltpu.VMEM((WIN, SLOT), jnp.bfloat16),
            pltpu.VMEM((LHS, SLOT), jnp.bfloat16),
            pltpu.VMEM((NB, NB), jnp.float32),
            pltpu.VMEM((NB, NB), jnp.float32),
            pltpu.VMEM((CLS, 8, 128), jnp.float32),
            pltpu.VMEM((FEAT, 8, 128), jnp.float32),
            dma((2,)),
            dma((2,)),
            dma((NPAN,)),
            dma((NPAN,)),
            dma((NPAN, 6)),
            dma((NPAN, 6)),
            dma((NPAN, 5)),
            dma((NPAN, 5)),
            dma((3, 3, 2)),
            dma((3, 3, 2)),
            dma((4, 2)),
            dma((4, 2)),
            dma((2,)),
            dma((2,)),
            dma((2,)),
            dma((2,)),
            dma(()),
            dma(()),
        ],
        compiler_params=pltpu.CompilerParams(
            collective_id=0, has_side_effects=True, vmem_limit_bytes=44 * 2**20
        ),
        cost_estimate=pl.CostEstimate(flops=2 * 2048 * 4608 * 640, bytes_accessed=40 * 2**20, transcendentals=0),
    )(emb, lab, prev)


def finish_kernel(gram, panel, ssum, tsum, cnt, out, out_panel):
    inv = 1.0 / cnt[0:1, 0:1]
    r = pl.ds(pl.multiple_of(64 * pl.program_id(0), 64), 64)
    out[...] = gram[r, :] * inv - (tsum[r, 0:1] * inv) * (ssum[0:1, :] * inv)
    out_panel[...] = panel[r, :]


def finish(gram, panel, ssum, tsum, cnt):
    return pl.pallas_call(
        finish_kernel,
        grid=(TILE // 64,),
        out_shape=(
            jax.ShapeDtypeStruct((TILE, D), jnp.float32),
            jax.ShapeDtypeStruct((OWN, PANEL), jnp.float32),
        ),
        in_specs=[pl.BlockSpec(memory_space=pltpu.VMEM)] * 5,
        out_specs=(pl.BlockSpec((64, D), lambda i: (i, 0)), pl.BlockSpec((64, PANEL), lambda i: (i, 0))),
        compiler_params=pltpu.CompilerParams(vmem_limit_bytes=16 * 2**20),
    )(gram, panel, ssum, tsum, cnt)


def body(embeddings, labels, previous):
    gram, panel, ssum, tsum, cnt = exchange(embeddings, labels.reshape(1, -1), previous[0])
    tile, panel = finish(gram, panel, ssum, tsum, cnt)
    return tile.T[None], panel[None]


def solution(mesh):
    return jax.shard_map(
        body,
        mesh=mesh,
        in_specs=(P(("cls", "feat"), None), P(("cls", "feat"), None), P("cls", "feat", None)),
        out_specs=(P("cls", None, "feat"), P("cls", "feat", None)),
        check_vma=False,
    )
```

```python
import functools

import jax
import jax.numpy as jnp
from jax import lax
from jax.experimental import pallas as pl
from jax.experimental.pallas import tpu as pltpu
from jax.sharding import PartitionSpec as P

MESH = pl.DeviceIdType.MESH
HI = lax.Precision.HIGHEST
D = 4608
CAP = 16
CLS = 16
FEAT = 8
PW = 2560
QW = D - PW
SLOT = CAP * CLS
HALF = SLOT // 2
TILE = D // FEAT
WIN = 640
PANEL = 1152
OWN = 576
ROWS = 1792
NB = 128
COLS = 384
NPAN = 3
PIECE = (144, 96, 48)
LPW = 128
LHS = TILE + 16


def dot_t(a, b):
    return lax.dot_general(a, b, (((1,), (1,)), ((), ())), precision=HI, preferred_element_type=jnp.float32)


def diag_inverse(W, r0, SA, SM):
    SA[...] = W[pl.ds(r0, NB), pl.ds(r0, NB)]
    row = lax.broadcasted_iota(jnp.int32, (NB, NB), 0)
    col = lax.broadcasted_iota(jnp.int32, (NB, NB), 1)
    SM[...] = jnp.where(row == col, 1.0, 0.0).astype(jnp.float32)
    sub = lax.broadcasted_iota(jnp.int32, (8, NB), 0)
    for g in range(NB // 8):
        lo = 8 * g
        pa = SA[lo : lo + 8, :]
        pm = SM[lo : lo + 8, :]
        cols = [jnp.broadcast_to(pa[:, lo + t : lo + t + 1], (8, NB)) for t in range(8)]
        scale = jnp.zeros((8, NB), jnp.float32)
        invs, rows_a, rows_m, heads = [], [], [], []
        for t in range(8):
            heads.append([jnp.broadcast_to(cols[u][t : t + 1, :], (8, NB)) for u in range(8)])
            rows_a.append(jnp.broadcast_to(pa[t : t + 1, :], (8, NB)))
            rows_m.append(jnp.broadcast_to(pm[t : t + 1, :], (8, NB)))
            invs.append(1.0 / heads[t][t])
            m = jnp.where(sub > t, cols[t] * invs[t], 0.0)
            scale = jnp.where(sub == t, heads[t][t], scale)
            for u in range(t + 1, 8):
                cols[u] = cols[u] - m * heads[t][u]
            pa = pa - m * rows_a[t]
            pm = pm - m * rows_m[t]
        SM[lo : lo + 8, :] = pm * lax.rsqrt(scale)
        for i in range(g + 1, NB // 8):
            r = slice(8 * i, 8 * i + 8)
            a = SA[r, :]
            b = SM[r, :]
            q = [jnp.broadcast_to(a[:, lo + t : lo + t + 1], (8, NB)) for t in range(8)]
            for t in range(8):
                m = q[t] * invs[t]
                a = a - m * rows_a[t]
                b = b - m * rows_m[t]
                for u in range(t + 1, 8):
                    q[u] = q[u] - m * heads[t][u]
            SA[r, :] = a
            SM[r, :] = b


def chol_step(W, k, SA, SM, hook):
    r0 = pl.multiple_of(k * NB, NB)
    b = lax.rem(k, 3)
    s = k // 3
    for st in (1, 2):

        @pl.when((b == 0) & (s == st))
        def _():
            c0 = 384 * st

            def body(i, _):
                r = pl.multiple_of(c0 + i * 128, 128)
                acc = W[pl.ds(r, 128), c0 : c0 + 384]
                for q in range(st):
                    acc = acc - dot_t(
                        W[pl.ds(r, 128), 384 * q : 384 * q + 384], W[c0 : c0 + 384, 384 * q : 384 * q + 384]
                    )
                W[pl.ds(r, 128), c0 : c0 + 384] = acc
                return 0

            lax.fori_loop(0, (ROWS - c0) // 128, body, 0)

    diag_inverse(W, r0, SA, SM)
    hook(0)

    def tb(i, _):
        r = pl.multiple_of(i * 256, 256)
        W[pl.ds(r, 256), pl.ds(r0, NB)] = dot_t(W[pl.ds(r, 256), pl.ds(r0, NB)], SM[...])
        return 0

    lax.fori_loop((k + 1) // 2, ROWS // 256, tb, 0)
    for bb in (0, 1):

        @pl.when(b == bb)
        def _():
            n = 256 - 128 * bb

            def ub(i, _):
                r = pl.multiple_of(i * 256, 256)
                c1 = pl.multiple_of(r0 + NB, NB)
                W[pl.ds(r, 256), pl.ds(c1, n)] = W[pl.ds(r, 256), pl.ds(c1, n)] - dot_t(
                    W[pl.ds(r, 256), pl.ds(r0, NB)], W[pl.ds(c1, n), pl.ds(r0, NB)]
                )
                return 0

            lax.fori_loop((k + 1) // 2, ROWS // 256, ub, 0)


def kernel(
    emb, lab, prev,
    gram, panel, ssum, tsum, cnt,
    E, STP, STQ, CST, GP, GQ, W, XT, TT, LT, SA, SM, C1, C2,
    p1r, p1s, lr, ls, lxs, lxr, lzs, lzr, xs, xr, zs, zr, ps, pr, cr, cs, own_sem, emb_sem,
):
    c = lax.axis_index("cls")
    f = lax.axis_index("feat")
    x = lax.rem(f, 4)
    zoff = f - x
    zmate = 4 - zoff
    mate = x + zmate
    zhi = lax.rem(c // 2, 2)

    def at_x(d, z):
        return z + lax.rem(x + d, 4)

    right, left, far = at_x(1, zoff), at_x(3, zoff), at_x(2, zoff)

    bar = pltpu.get_barrier_semaphore()

    def sig(cc, ff):
        pl.semaphore_signal(bar, inc=1, device_id=(cc, ff), device_id_type=MESH)

    def sig_cls(cc, _):
        @pl.when(cc != c)
        def _():
            sig(cc, f)

        sig(cc, mate)
        return 0

    emb_copy = pltpu.make_async_copy(emb, E, emb_sem)
    emb_copy.start()
    own_copy = pltpu.make_async_copy(prev, W.at[PANEL : PANEL + OWN, :], own_sem)
    own_copy.start()
    lax.fori_loop(0, CLS, sig_cls, 0)
    for d in (1, 2, 3):
        sig(c, at_x(d, zoff))
        sig(c, at_x(d, zmate))
    n = emb.shape[0]
    label = lab[...].astype(jnp.float32)
    onehot = (lax.broadcasted_iota(jnp.int32, (CLS, n), 0).astype(jnp.float32) == label).astype(jnp.float32)
    t0 = lax.broadcasted_iota(jnp.int32, (n, n), 0)
    t1 = lax.broadcasted_iota(jnp.int32, (n, n), 1)
    ahead = jnp.dot(
        onehot.astype(jnp.bfloat16), (t0 < t1).astype(jnp.float32).astype(jnp.bfloat16), preferred_element_type=jnp.float32
    )
    place = label * CAP + jnp.sum(ahead * onehot, axis=0, keepdims=True)
    pick = (lax.broadcasted_iota(jnp.int32, (SLOT, n), 0).astype(jnp.float32) == place).astype(jnp.float32)
    pick = pick.astype(jnp.bfloat16)
    counts = jnp.sum(onehot, axis=1, keepdims=True)
    for i in range(CLS):
        CST[i] = jnp.broadcast_to(counts[i : i + 1, :], (8, 128))
    emb_copy.wait()

    def choose(ref, w, c0):
        for i in range(w // 512):
            cols = slice(512 * i, 512 * (i + 1))
            chosen = jnp.dot(pick, E[:, c0 + 512 * i : c0 + 512 * (i + 1)], preferred_element_type=jnp.float32)
            ref[:, cols] = chosen.astype(jnp.bfloat16)

    choose(STQ, QW, PW)
    pl.semaphore_wait(bar, 37)

    def put(src, dst, dev, ssem, rsem):
        pltpu.make_async_remote_copy(
            src_ref=src, dst_ref=dst, send_sem=ssem, recv_sem=rsem, device_id=dev, device_id_type=MESH
        ).start()

    def wait(ref, sem):
        pltpu.make_async_copy(ref, ref, sem).wait()

    def put_same(ref, ff, ssem, rsem):
        put(ref, ref, (c, ff), ssem, rsem)

    def piece(j, i, lo=0, hi=COLS):
        r = pl.multiple_of(COLS * j + PIECE[j] * i, 8)
        return W.at[pl.ds(r, PIECE[j]), COLS * j + lo : COLS * j + hi]

    for src in (0, 1):

        @pl.when(f == src)
        def _():
            for j in range(NPAN):
                for i in range(FEAT):
                    r = COLS * j + PIECE[j] * i
                    if r // OWN != src:
                        continue
                    r = r - OWN * src
                    ref = prev.at[r : r + PIECE[j], COLS * j : COLS * (j + 1)]
                    if i == src:
                        pltpu.make_async_copy(ref, piece(j, i), lr.at[j]).start()
                    else:
                        put(ref, piece(j, i), (c, i), ls.at[j], lr.at[j])

    def rows_of(ref, cc):
        return ref.at[pl.ds(pl.multiple_of(CAP * cc, CAP), CAP), :]

    def route(cc, _):
        same = lax.rem(cc // 2, 2) == zhi
        g = jnp.where(same, f, mate)
        r = pl.multiple_of(CAP * c, CAP)
        dq = GQ.at[g, pl.ds(r, CAP), :]

        @pl.when(cc == c)
        def _():
            pltpu.make_async_copy(rows_of(STQ, cc), dq, p1r.at[0]).start()
            pltpu.make_async_copy(CST.at[cc], C1.at[c], cr.at[0]).start()

        @pl.when(cc != c)
        def _():
            put(rows_of(STQ, cc), dq, (cc, g), p1s.at[0], p1r.at[0])
            put(CST.at[cc], C1.at[c], (cc, f), cs.at[0], cr.at[0])

        return 0

    lax.fori_loop(0, CLS, route, 0)
    choose(STP, PW, 0)

    def route_p(cc, _):
        same = lax.rem(cc // 2, 2) == zhi
        g = jnp.where(same, f, mate)
        r = pl.multiple_of(CAP * c, CAP)
        dp = GP.at[g, pl.ds(r, CAP), :]

        @pl.when(cc == c)
        def _():
            pltpu.make_async_copy(rows_of(STP, cc), dp, p1r.at[1]).start()

        @pl.when(cc != c)
        def _():
            put(rows_of(STP, cc), dp, (cc, g), p1s.at[1], p1r.at[1])

        return 0


    def zero(i, _):
        gram[:, pl.ds(pl.multiple_of(512 * i, 512), 512)] = jnp.zeros((TILE, 512), jnp.float32)
        return 0

    lax.fori_loop(0, D // 512, zero, 0)
    ssum[...] = jnp.zeros_like(ssum)
    tsum[...] = jnp.zeros_like(tsum)
    LT[TILE:, :] = jnp.ones((LHS - TILE, SLOT), jnp.bfloat16)
    W[PANEL + OWN :, :] = jnp.zeros((ROWS - PANEL - OWN, PANEL), jnp.float32)

    along_x = ((0, right), (1, left), (2, far))
    from_x = ((0, 3), (1, 1), (2, 2))

    def lead_a(j):
        wait(piece(j, f), lr.at[j])
        put_same(piece(j, f, 0, LPW), mate, lzs.at[j, 0], lzr.at[j, 0])
        for d, ff in along_x:
            put_same(piece(j, f), ff, lxs.at[j, d], lxr.at[j, d])
        put_same(piece(j, f, LPW), mate, lzs.at[j, 1], lzr.at[j, 1])

    def lead_b(j):
        wait(piece(j, mate, 0, LPW), lzr.at[j, 0])
        for d, ff in along_x:
            put_same(piece(j, mate, 0, LPW), ff, lxs.at[j, 3 + d], lxr.at[j, 3 + d])

    def lead_c(j):
        for d, off in from_x:
            wait(piece(j, at_x(off, zoff)), lxr.at[j, d])
            put_same(piece(j, at_x(off, zoff), LPW), mate, lzs.at[j, 2 + d], lzr.at[j, 2 + d])

    def lead_d(j):
        wait(piece(j, mate, LPW), lzr.at[j, 1])
        for d, off in from_x:
            wait(piece(j, at_x(off, zmate), 0, LPW), lxr.at[j, 3 + d])
            wait(piece(j, at_x(off, zmate), LPW), lzr.at[j, 2 + d])
        wait(piece(j, f, 0, LPW), lzs.at[j, 0])
        wait(piece(j, f, LPW), lzs.at[j, 1])
        for d in range(3):
            wait(piece(j, f), lxs.at[j, d])
            wait(piece(j, mate, 0, LPW), lxs.at[j, 3 + d])
            wait(piece(j, f, LPW), lzs.at[j, 2 + d])

    def block(st, xoff, h):
        ref = GQ if st == 0 else GP
        slot = at_x(xoff, zmate if st == 2 else zoff)
        return ref.at[slot, HALF * h : HALF * (h + 1), :]

    def send_own(st):
        for h in (0, 1):
            put_same(block(st, 0, h), right, xs.at[st, 0, h], xr.at[st, 0, h])
            put_same(block(st, 0, 1 - h), left, xs.at[st, 1, 1 - h], xr.at[st, 1, 1 - h])

    def to_mate(d, h):
        b = GQ.at[at_x(d, zoff), HALF * h : HALF * (h + 1), :]
        put_same(b, mate, zs.at[d, h], zr.at[d, h])

    def start_q():
        wait(GQ.at[f], p1r.at[0])
        lax.fori_loop(0, CLS, route_p, 0)
        to_mate(0, 0)
        to_mate(0, 1)
        send_own(0)

    def start_p():
        wait(GP.at[f], p1r.at[1])
        for h in (0, 1):
            put_same(block(1, 0, h), mate, ps.at[h], pr.at[h])
        send_own(1)

    def start_mate_p():
        for h in (0, 1):
            wait(block(2, 0, h), pr.at[h])
            put_same(block(2, 0, h), right if h == 0 else left, xs.at[2, h, h], xr.at[2, h, h])
        for h in (0, 1):
            put_same(block(2, 0, h), left if h == 0 else right, xs.at[2, 1 - h, h], xr.at[2, 1 - h, h])

    def forward(st, last):
        if not last:
            wait(block(st, 3, 0), xr.at[st, 0, 0])
            put_same(block(st, 3, 0), right, xs.at[st, 2, 0], xr.at[st, 2, 0])
            wait(block(st, 1, 1), xr.at[st, 1, 1])
            put_same(block(st, 1, 1), left, xs.at[st, 2, 1], xr.at[st, 2, 1])
            if st == 0:
                to_mate(3, 0)
                to_mate(1, 1)
        else:
            wait(block(st, 3, 1), xr.at[st, 0, 1])
            wait(block(st, 1, 0), xr.at[st, 1, 0])
            if st == 0:
                to_mate(3, 1)
                to_mate(1, 0)

    def far_in(st):
        for h in (0, 1):
            wait(block(st, 2, h), xr.at[st, 2, h])
            if st == 0:
                to_mate(2, h)

    def mate_q(d):
        for h in (0, 1):
            wait(GQ.at[at_x(d, zmate), HALF * h : HALF * (h + 1), :], zr.at[d, h])

    def count():
        wait(C1, cr.at[0])
        C2[f] = jnp.sum(C1[...], axis=0)
        for d in (1, 2, 3):
            put_same(C2.at[f], at_x(d, zoff), cs.at[1], cr.at[1])
        for d in (0, 1, 2, 3):
            put_same(C2.at[f], at_x(d, zmate), cs.at[1], cr.at[1])

    base = (9 * f) // 2
    half_tile = 64 * lax.rem(f, 2)

    def gram_slot(s):
        for i in range(WIN // 128):
            j = base + i
            dst = slice(128 * i, 128 * (i + 1))

            @pl.when(j < PW // 128)
            def _():
                XT[:, dst] = GP[s, :, pl.ds(pl.multiple_of(128 * j, 128), 128)]

            @pl.when(j >= PW // 128)
            def _():
                XT[:, dst] = GQ[s, :, pl.ds(pl.multiple_of(128 * (j - PW // 128), 128), 128)]

        TT[...] = XT[...].T
        LT[:TILE, :] = TT[pl.ds(pl.multiple_of(half_tile, 64), TILE), :]
        tsum[...] += jnp.dot(LT[:TILE, :], jnp.ones((SLOT, 128), jnp.bfloat16), preferred_element_type=jnp.float32)
        for ref, n, r0 in ((GP, PW, 0), (GQ, QW, PW)):

            def chunk(i, _):
                q = 512 * i
                r = pl.ds(r0 + q, 512)
                acc = jnp.dot(LT[...], ref[s, :, pl.ds(q, 512)], preferred_element_type=jnp.float32)
                gram[:, r] += acc[:TILE]
                ssum[:, r] += acc[TILE:]
                return 0

            for i in range(n // 512):
                chunk(i, 0)

    for j in range(NPAN):
        lead_a(j)
    lead_b(0)
    start_q()
    lead_c(0)
    start_p()
    lead_d(0)
    own_copy.wait()

    events = {
        0: [lambda: lead_b(1), lambda: lead_b(2)],
        1: [lambda: lead_c(1), lambda: lead_c(2), count],
        3: [lambda: forward(0, False)],
        4: [lambda: lead_d(1), lambda: forward(0, True)],
        5: [lambda: lead_d(2)],
        6: [start_mate_p],
        7: [lambda: far_in(0)],
        10: [lambda: mate_q(0)],
        11: [lambda: forward(1, False)],
        13: [lambda: forward(1, True)],
        15: [lambda: forward(2, False)],
    }

    def hooks(k, place):
        for at, evs in events.items():
            if at % 2 == place:

                @pl.when(k == at // 2)
                def _():
                    for ev in evs:
                        ev()

    def step(k, _):
        chol_step(W, k, SA, SM, functools.partial(hooks, k))
        hooks(k, 1)

        @pl.when((k == 1) | (k == 6) | (k >= 7))
        def _():
            gram_slot(jnp.where(k == 1, f, jnp.where(k == 6, mate, jnp.where(k == 7, right, left))))

        return 0

    lax.fori_loop(0, PANEL // NB, step, 0)
    panel[...] = W[PANEL : PANEL + OWN, :]

    far_in(1)

    def last(n, _):
        @pl.when(n == 1)
        def _():
            forward(2, True)
            mate_q(1)

        @pl.when(n == 2)
        def _():
            mate_q(3)

        @pl.when(n == 3)
        def _():
            far_in(2)
            mate_q(2)

        d = jnp.where(n == 1, 1, jnp.where(n == 2, 3, 2))
        gram_slot(at_x(d, jnp.where(n == 0, zoff, zmate)))
        return 0

    lax.fori_loop(0, 4, last, 0)

    wait(C2.at[0:7], cr.at[1])
    cnt[...] = jnp.sum(C2[...], axis=0)

    for src, rows in ((0, (432, 96, 0)), (1, (576, 576, 336))):

        @pl.when(f == src)
        def _():
            for j in range(NPAN):
                if rows[j]:
                    wait(prev.at[0 : rows[j], 0:COLS], ls.at[j])

    wait(STQ.at[0 : 15 * CAP, :], p1s.at[0])
    wait(STP.at[0 : 15 * CAP, :], p1s.at[1])
    wait(CST.at[0:15], cs.at[0])
    wait(C2.at[0:7], cs.at[1])
    for h in (0, 1):
        wait(block(1, 0, h), ps.at[h])
    for st in range(3):
        for d in range(3):
            for h in (0, 1):
                wait(block(st, 0, h), xs.at[st, d, h])
    for d in range(4):
        for h in (0, 1):
            wait(GQ.at[f, HALF * h : HALF * (h + 1), :], zs.at[d, h])


def exchange(emb, lab, prev):
    dma = pltpu.SemaphoreType.DMA
    any_space = pl.BlockSpec(memory_space=pl.ANY)
    vmem = pl.BlockSpec(memory_space=pltpu.VMEM)
    return pl.pallas_call(
        kernel,
        out_shape=(
            pltpu.VMEM((TILE, D), jnp.float32),
            pltpu.VMEM((OWN, PANEL), jnp.float32),
            pltpu.VMEM((LHS - TILE, D), jnp.float32),
            pltpu.VMEM((TILE, 128), jnp.float32),
            pltpu.VMEM((8, 128), jnp.float32),
        ),
        in_specs=[any_space, vmem, any_space],
        out_specs=(vmem,) * 5,
        scratch_shapes=[
            pltpu.VMEM((128, D), jnp.bfloat16),
            pltpu.VMEM((SLOT, PW), jnp.bfloat16),
            pltpu.VMEM((SLOT, QW), jnp.bfloat16),
            pltpu.VMEM((CLS, 8, 128), jnp.float32),
            pltpu.VMEM((FEAT, SLOT, PW), jnp.bfloat16),
            pltpu.VMEM((FEAT, SLOT, QW), jnp.bfloat16),
            pltpu.VMEM((ROWS, PANEL), jnp.float32),
            pltpu.VMEM((SLOT, WIN), jnp.bfloat16),
            pltpu.VMEM((WIN, SLOT), jnp.bfloat16),
            pltpu.VMEM((LHS, SLOT), jnp.bfloat16),
            pltpu.VMEM((NB, NB), jnp.float32),
            pltpu.VMEM((NB, NB), jnp.float32),
            pltpu.VMEM((CLS, 8, 128), jnp.float32),
            pltpu.VMEM((FEAT, 8, 128), jnp.float32),
            dma((2,)),
            dma((2,)),
            dma((NPAN,)),
            dma((NPAN,)),
            dma((NPAN, 6)),
            dma((NPAN, 6)),
            dma((NPAN, 5)),
            dma((NPAN, 5)),
            dma((3, 3, 2)),
            dma((3, 3, 2)),
            dma((4, 2)),
            dma((4, 2)),
            dma((2,)),
            dma((2,)),
            dma((2,)),
            dma((2,)),
            dma(()),
            dma(()),
        ],
        compiler_params=pltpu.CompilerParams(
            collective_id=0, has_side_effects=True, vmem_limit_bytes=44 * 2**20
        ),
        cost_estimate=pl.CostEstimate(flops=2 * 2048 * 4608 * 640, bytes_accessed=40 * 2**20, transcendentals=0),
    )(emb, lab, prev)


def finish_kernel(gram, panel, ssum, tsum, cnt, out, out_panel):
    inv = 1.0 / cnt[0:1, 0:1]
    r = pl.ds(pl.multiple_of(64 * pl.program_id(0), 64), 64)
    out[...] = gram[r, :] * inv - (tsum[r, 0:1] * inv) * (ssum[0:1, :] * inv)
    out_panel[...] = panel[r, :]


def finish(gram, panel, ssum, tsum, cnt):
    return pl.pallas_call(
        finish_kernel,
        grid=(TILE // 64,),
        out_shape=(
            jax.ShapeDtypeStruct((TILE, D), jnp.float32),
            jax.ShapeDtypeStruct((OWN, PANEL), jnp.float32),
        ),
        in_specs=[pl.BlockSpec(memory_space=pltpu.VMEM)] * 5,
        out_specs=(pl.BlockSpec((64, D), lambda i: (i, 0)), pl.BlockSpec((64, PANEL), lambda i: (i, 0))),
        compiler_params=pltpu.CompilerParams(vmem_limit_bytes=16 * 2**20),
    )(gram, panel, ssum, tsum, cnt)


def body(embeddings, labels, previous):
    gram, panel, ssum, tsum, cnt = exchange(embeddings, labels.reshape(1, -1), previous[0])
    tile, panel = finish(gram, panel, ssum, tsum, cnt)
    return tile.T[None], panel[None]


def solution(mesh):
    return jax.shard_map(
        body,
        mesh=mesh,
        in_specs=(P(("cls", "feat"), None), P(("cls", "feat"), None), P("cls", "feat", None)),
        out_specs=(P("cls", None, "feat"), P("cls", "feat", None)),
        check_vma=False,
    )
```
